32 devices in a mesh: atoms: 16 (over z, y, core), kvec: 2 (over x).
Axes of the slice: x: 2, y: 2, z: 4, core: 2. Of those that a mesh axis runs over, the one named last changes fastest.
Arguments:
- particle_traits: bfloat16 [65536, 256], P('atoms'), may hold values from -6 to 6
- particle_coordinates: float32 [3, 65536], P(None, 'atoms'), may hold values from 0 to 24
- kspace_vectors: float32 [3, 4096], P(None, 'kvec'), may hold values from -1.5 to 1.5
- learned_kspace_filter: float32 [4096, 256], P('kvec'), may hold values from -4 to 4
- spatial_home: int32 [16, 4096], P('atoms'), may hold values from 0 to 4095, each once within a row
- following_halo_lines: int32 [16, 512], P('atoms'), may hold values from 0 to 4095
- previous_halo_lines: int32 [16, 512], P('atoms'), may hold values from 0 to 4095
- sender_projection: bfloat16 [256, 256], replicated, may hold values from -0.375 to 0.375
- receiver_projection: bfloat16 [256, 256], replicated, may hold values from -0.375 to 0.375
- pair_channel_mapping: bfloat16 [196, 256], replicated, may hold values from -0.375 to 0.375
- vertex_rescaling_gain: float32 [256], replicated, may hold values from 0.1 to 1.9
- link_sender_line: int32 [131072], P(('atoms', 'kvec')), may hold values from 0 to 5119
- link_receiver_particle: int32 [131072], P(('atoms', 'kvec')), may hold values from 0 to 4095
- active_link_tally: int32 [32], P(('atoms', 'kvec')), may hold values from 32 to 4096, as said below
Outputs:
- orbital_blocks: bfloat16 [196, 131072], P(None, ('atoms', 'kvec'))
- partitioned: bfloat16 [65536, 256], P('atoms')
The draws below stay inside these ranges and needn't reach their ends.
Inputs may be any that keep to these rules, and one draw needn't show every extreme that they name: `spatial_home`: each row of destination orders one device's 4096 atoms; every device sends exactly 256 atoms to every partition. `following_halo_lines`: rows of the sending partition. `previous_halo_lines`: rows of the sending partition. `link_sender_line`: A table row: the partition's 4096 own atoms, then 512 ghosts from the previous partition, then 512 from the next. `active_link_tally`: A multiple of 32; the used edges are the first ones of a device's list; some device uses all 4096 slots.
All inputs are finite; a program needn't handle non-finite values.
Results may differ from the reference program's by a relative error of at most 0.01.
Values may be sent and summed in bfloat16 or wider, within the bound.
A program may use at most 64 MiB of HBM per device.

```python
import math
import jax
import jax.numpy as jnp
from jax import lax

C = 256
KSPACE_NUMBER = 4096
ORB = 196
A_DEV = 4096
E_DEV = 4096
G = 512
GRP = 256
ATOMS = 65536
EDGES = 131072
N_ATOMS = 16
N_KVEC = 2
DEVICES = 32


def draw_active_link_tally(key, part):
    first_key = jax.random.fold_in(key, 11)
    second_key = jax.random.fold_in(key, 23)
    counts = jax.random.randint(first_key, (DEVICES,), 1, E_DEV // 32 + 1) * 32
    full_dev = jax.random.randint(second_key, (), 0, DEVICES)
    return jnp.where(jnp.arange(DEVICES) == full_dev, E_DEV, counts).astype(jnp.int32)


def plant(result, own_key, least, high):
    longest = result.shape.index(max(result.shape))
    spots = []
    for shift in (0, 1):
        where = [jax.random.randint(jax.random.fold_in(own_key, axis), (), 0, length) for axis, length in enumerate(result.shape)]
        where[longest] = (where[longest] + shift) % result.shape[longest]
        spots.append(tuple(where))
    return result.at[spots[0]].set(least).at[spots[1]].set(high)


def steps_of(key, extent, cuts, smallest, high):
    def one(position, shards_of):
        steps = jax.random.uniform(jax.random.fold_in(jax.random.fold_in(key, 6), position), (shards_of,), jnp.float32, smallest / len(cuts), high / len(cuts))
        return jnp.repeat(jnp.exp(steps), extent[position] // shards_of).reshape((-1,) + (1,) * (len(extent) - position - 1))

    loudness = one(*cuts[0])
    for cut in cuts[1:]:
        loudness = loudness * one(*cut)
    return loudness


def bell_draw(own_key, dims, spread, most, pieces=(), kind=jnp.bfloat16):
    level = steps_of(own_key, dims, pieces, -0.22, 0.18) if pieces else 1.0
    entries = jax.random.normal(own_key, dims, jnp.float32) * spread * level
    return jnp.minimum(jnp.maximum(entries, -most), most).astype(kind)


def setup_inputs(seed: int = 0) -> dict:
    seeds = jax.random.split(jax.random.key(seed), 15)
    return {
        "particle_traits": bell_draw(seeds[0], (ATOMS, C), 1.0, 6.0, ((0, 16),)),
        "particle_coordinates": jnp.clip(24.0 * jax.random.uniform(seeds[1], (3, ATOMS), jnp.float32) ** steps_of(seeds[1], (3, ATOMS), ((1, 16),), -0.2, 0.2), 0.0, 24.0),
        "kspace_vectors": jnp.clip(jax.random.uniform(seeds[2], (3, KSPACE_NUMBER), jnp.float32, -1.5, 1.5) * steps_of(seeds[2], (3, KSPACE_NUMBER), ((1, 2),), -0.4, 0.0), -1.5, 1.5),
        "learned_kspace_filter": bell_draw(seeds[3], (KSPACE_NUMBER, C), 1.0, 4.0, ((0, 2),), jnp.float32),
        "spatial_home": jax.vmap(lambda own: jax.random.permutation(own, A_DEV))(jax.random.split(seeds[4], N_ATOMS)).reshape((N_ATOMS, A_DEV)).astype(jnp.int32),
        "following_halo_lines": plant(jax.random.randint(seeds[5], (N_ATOMS, G), 0, A_DEV), jax.random.fold_in(seeds[5], 1), 0, A_DEV - 1).astype(jnp.int32),
        "previous_halo_lines": plant(jax.random.randint(seeds[6], (N_ATOMS, G), 0, A_DEV), jax.random.fold_in(seeds[6], 1), 0, A_DEV - 1).astype(jnp.int32),
        "sender_projection": bell_draw(seeds[7], (C, C), C ** -0.5, 0.375),
        "receiver_projection": bell_draw(seeds[8], (C, C), C ** -0.5, 0.375),
        "pair_channel_mapping": bell_draw(seeds[9], (ORB, C), C ** -0.5, 0.375),
        "vertex_rescaling_gain": jnp.clip(1.0 + 0.18 * jax.random.normal(seeds[10], (C,), jnp.float32), 0.1, 1.9),
        "link_sender_line": plant(jax.random.randint(seeds[11], (EDGES,), 0, A_DEV + 2 * G), jax.random.fold_in(seeds[11], 1), 0, (A_DEV + 2 * G) - 1).astype(jnp.int32),
        "link_receiver_particle": plant(jax.random.randint(seeds[12], (EDGES,), 0, A_DEV), jax.random.fold_in(seeds[12], 1), 0, A_DEV - 1).astype(jnp.int32),
        "active_link_tally": draw_active_link_tally(jax.random.fold_in(seeds[14], 71), 0),
    }


def reference(particle_traits, particle_coordinates, kspace_vectors, learned_kspace_filter, spatial_home, following_halo_lines, previous_halo_lines, sender_projection, receiver_projection, pair_channel_mapping, vertex_rescaling_gain, link_sender_line, link_receiver_particle, active_link_tally):
    norm_scale = 1.0 / math.sqrt(ATOMS * KSPACE_NUMBER)
    kspace_group = min(512, KSPACE_NUMBER)
    nblocks = KSPACE_NUMBER // kspace_group

    def kspace_stride(summed_increment, kspace_group_number):
        kspace_portion = lax.dynamic_slice_in_dim(kspace_vectors, kspace_group_number * kspace_group, kspace_group, 1)
        filter_portion = lax.dynamic_slice_in_dim(learned_kspace_filter, kspace_group_number * kspace_group, kspace_group, 0)
        wave_arguments = particle_coordinates[0][:, None] * kspace_portion[0][None, :] + particle_coordinates[1][:, None] * kspace_portion[1][None, :]
        wave_arguments = wave_arguments + particle_coordinates[2][:, None] * kspace_portion[2][None, :]
        cosine_vals = jnp.cos(wave_arguments).astype(jnp.bfloat16)
        sine_vals = jnp.sin(wave_arguments).astype(jnp.bfloat16)
        struct_cos = jnp.dot(cosine_vals.T, particle_traits, preferred_element_type=jnp.float32)
        struct_sin = jnp.dot(sine_vals.T, particle_traits, preferred_element_type=jnp.float32)
        filt_cos = (filter_portion * struct_cos * norm_scale).astype(jnp.bfloat16)
        filt_sin = (filter_portion * struct_sin * norm_scale).astype(jnp.bfloat16)
        summed_increment = summed_increment + jnp.dot(cosine_vals, filt_cos, preferred_element_type=jnp.float32)
        summed_increment = summed_increment + jnp.dot(sine_vals, filt_sin, preferred_element_type=jnp.float32)
        return (summed_increment, None)
    summed_increment, _ = lax.scan(kspace_stride, jnp.zeros((ATOMS, C), jnp.float32), jnp.arange(nblocks, dtype=jnp.int32))
    refreshed = particle_traits.astype(jnp.float32) + jax.nn.silu(summed_increment)
    node = (refreshed * lax.rsqrt(lax.optimization_barrier(jnp.mean(refreshed * refreshed, axis=-1, keepdims=True)) + 1e-06) * vertex_rescaling_gain).astype(jnp.bfloat16)
    source_dev = jnp.arange(ATOMS, dtype=jnp.int32) // A_DEV
    slot_ids = spatial_home.reshape(-1).astype(jnp.int32)
    target_rows = slot_ids // GRP * A_DEV + source_dev * GRP + slot_ids % GRP
    partitioned = jnp.zeros((ATOMS, C), jnp.bfloat16).at[target_rows].set(node)
    left_proj = jnp.dot(partitioned, sender_projection, preferred_element_type=jnp.float32).astype(jnp.bfloat16)
    right_proj = jnp.dot(partitioned, receiver_projection, preferred_element_type=jnp.float32).astype(jnp.bfloat16)
    edge_ids = jnp.arange(EDGES, dtype=jnp.int32)
    part_ids = edge_ids // (E_DEV * N_KVEC)
    lower_part = (part_ids - 1) % N_ATOMS
    upper_part = (part_ids + 1) % N_ATOMS
    own_rows = part_ids * A_DEV + link_sender_line
    lower_rows = lower_part * A_DEV + following_halo_lines[lower_part, jnp.clip(link_sender_line - A_DEV, 0, G - 1)]
    upper_rows = upper_part * A_DEV + previous_halo_lines[upper_part, jnp.clip(link_sender_line - A_DEV - G, 0, G - 1)]
    source_rows = jnp.where(link_sender_line < A_DEV, own_rows, jnp.where(link_sender_line < A_DEV + G, lower_rows, upper_rows))
    target_idx = part_ids * A_DEV + link_receiver_particle
    in_use = edge_ids % E_DEV < active_link_tally[edge_ids // E_DEV]

    def expand(packed):
        src_rows, dst_rows, used = packed
        pair = (left_proj[src_rows].astype(jnp.float32) * right_proj[dst_rows].astype(jnp.float32)).astype(jnp.bfloat16)
        orb_block = jnp.dot(pair_channel_mapping, pair.T, preferred_element_type=jnp.float32)
        return jnp.where(used[None, :], orb_block, 0.0).astype(jnp.bfloat16)
    blocks = lax.map(expand, (source_rows.reshape(DEVICES, E_DEV), target_idx.reshape(DEVICES, E_DEV), in_use.reshape(DEVICES, E_DEV)))
    orbital_blocks = jnp.transpose(blocks, (1, 0, 2)).reshape(ORB, EDGES)
    return (orbital_blocks, partitioned)
```

```python
import functools
import math

import jax
import jax.numpy as jnp
from jax import lax
from jax.experimental import pallas as pl
from jax.experimental.pallas import tpu as pltpu
from jax.sharding import PartitionSpec as P

F32 = jnp.float32
BF16 = jnp.bfloat16
ROUNDER = 12582912.0

def even_poly(function, count):
    nodes = [0.125 + 0.125 * math.cos(math.pi * (i + 0.5) / count) for i in range(count)]
    table = [function(u) for u in nodes]
    for level in range(1, count):
        for i in range(count - 1, level - 1, -1):
            table[i] = (table[i] - table[i - 1]) / (nodes[i] - nodes[i - level])
    coeffs = [table[-1]]
    for i in range(count - 2, -1, -1):
        shifted = [0.0] + coeffs
        scaled = [-nodes[i] * c for c in coeffs] + [0.0]
        coeffs = [a + b for a, b in zip(shifted, scaled)]
        coeffs[0] += table[i]
    return coeffs


SIN_POLY = even_poly(lambda u: math.sqrt(2.0) * math.sin(math.pi * math.sqrt(u)) / math.sqrt(u), 4)
COS_POLY = even_poly(lambda u: math.sqrt(2.0) * math.cos(math.pi * math.sqrt(u)), 4)


def horner(coeffs, u):
    total = coeffs[-1]
    for c in coeffs[-2::-1]:
        total = total * u + c
    return total


def cos_sin(turns):
    r = turns - ((turns + ROUNDER) - ROUNDER)
    u = r * r
    s = r * horner(SIN_POLY, u)
    c = horner(COS_POLY, u)
    return (1.0 - s * s).astype(BF16), (s * c).astype(BF16)


def sort_kernel(ids_ref, coords_ref, feat_ref, feat_out, coords_out):
    rows = feat_out.shape[0]
    slots = pl.program_id(0) * rows + lax.broadcasted_iota(jnp.int32, (rows, 1), 0)
    pick = jnp.where(slots == ids_ref[...], 1.0, 0.0).astype(BF16)
    feat_out[...] = jnp.dot(pick, feat_ref[...], preferred_element_type=F32).astype(BF16)
    x = coords_ref[...]
    high = x.astype(BF16).astype(F32)
    rest = x - high
    mid = rest.astype(BF16).astype(F32)
    low = rest - mid
    parts = jnp.concatenate([high, mid, low], axis=0).astype(BF16)
    moved = lax.dot_general(parts, pick, (((1,), (1,)), ((), ())), preferred_element_type=F32)
    coords_out[...] = moved[0:8] + moved[8:16] + moved[16:24]


def sort_atoms(slot_ids, coords, feat):
    a_dev, chans = feat.shape
    block = min(512, a_dev)
    padded = jnp.concatenate([coords, jnp.zeros((8 - coords.shape[0], a_dev), F32)], axis=0)
    return pl.pallas_call(
        sort_kernel,
        grid=(a_dev // block,),
        in_specs=[
            pl.BlockSpec((1, a_dev), lambda i: (0, 0)),
            pl.BlockSpec((8, a_dev), lambda i: (0, 0)),
            pl.BlockSpec((a_dev, chans), lambda i: (0, 0)),
        ],
        out_specs=[
            pl.BlockSpec((block, chans), lambda i: (i, 0)),
            pl.BlockSpec((8, block), lambda i: (0, i)),
        ],
        out_shape=[
            jax.ShapeDtypeStruct((a_dev, chans), BF16),
            jax.ShapeDtypeStruct((8, a_dev), F32),
        ],
        compiler_params=pltpu.CompilerParams(vmem_limit_bytes=48 * 1024 * 1024),
        name="sort_atoms",
    )(slot_ids, padded, feat)


def waves_kernel(chunk, k_ref, x_ref, feat_ref, cos_ref, sin_ref, sums_ref):
    rows, atoms = cos_ref.shape
    sums_ref[...] = jnp.zeros_like(sums_ref)
    strip = 16

    def one_chunk(j, carry):
        lanes = pl.ds(pl.multiple_of(j * chunk, chunk), chunk)
        x0, x1, x2 = x_ref[0:1, lanes], x_ref[1:2, lanes], x_ref[2:3, lanes]
        coses, sines = [], []
        for top in range(0, rows, strip):
            k = k_ref[top : top + strip, :]
            turns = k[:, 0:1] * x0 + k[:, 1:2] * x1 + k[:, 2:3] * x2
            c, s = cos_sin(turns)
            coses.append(c)
            sines.append(s)
        c = jnp.concatenate(coses, axis=0)
        s = jnp.concatenate(sines, axis=0)
        cos_ref[:, lanes] = c
        sin_ref[:, lanes] = s
        f = feat_ref[lanes, :]
        sums_ref[0] += jnp.dot(c, f, preferred_element_type=F32)
        sums_ref[1] += jnp.dot(s, f, preferred_element_type=F32)
        return carry

    lax.fori_loop(0, atoms // chunk, one_chunk, 0)


def waves(k_turns, coords, feat):
    kspace = k_turns.shape[0]
    a_dev, chans = feat.shape
    block = min(256, kspace)
    return pl.pallas_call(
        functools.partial(waves_kernel, min(512, a_dev)),
        grid=(kspace // block,),
        in_specs=[
            pl.BlockSpec((block, k_turns.shape[1]), lambda i: (i, 0)),
            pl.BlockSpec((8, a_dev), lambda i: (0, 0)),
            pl.BlockSpec((a_dev, chans), lambda i: (0, 0)),
        ],
        out_specs=[
            pl.BlockSpec((block, a_dev), lambda i: (i, 0)),
            pl.BlockSpec((block, a_dev), lambda i: (i, 0)),
            pl.BlockSpec((2, block, chans), lambda i: (0, i, 0)),
        ],
        out_shape=[
            jax.ShapeDtypeStruct((kspace, a_dev), BF16),
            jax.ShapeDtypeStruct((kspace, a_dev), BF16),
            jax.ShapeDtypeStruct((2, kspace, chans), F32),
        ],
        compiler_params=pltpu.CompilerParams(vmem_limit_bytes=48 * 1024 * 1024),
        cost_estimate=pl.CostEstimate(
            flops=60 * kspace * a_dev + 4 * kspace * a_dev * chans,
            bytes_accessed=4 * kspace * a_dev,
            transcendentals=0,
        ),
        name="waves",
    )(k_turns, coords, feat)


def update_kernel(filt_ref, cos_ref, sin_ref, out_ref, turned):
    @pl.when(pl.program_id(0) == 0)
    def _():
        turned[0] = filt_ref[0].astype(F32).T.astype(BF16)
        turned[1] = filt_ref[1].astype(F32).T.astype(BF16)

    total = jnp.dot(turned[0], cos_ref[...], preferred_element_type=F32)
    total = total + jnp.dot(turned[1], sin_ref[...], preferred_element_type=F32)
    out_ref[...] = total.T.astype(BF16)


def update_rows(filt, cosine, sine):
    kspace, a_dev = cosine.shape
    chans = filt.shape[2]
    block = min(512, a_dev)
    return pl.pallas_call(
        update_kernel,
        grid=(a_dev // block,),
        in_specs=[
            pl.BlockSpec((2, kspace, chans), lambda i: (0, 0, 0)),
            pl.BlockSpec((kspace, block), lambda i: (0, i)),
            pl.BlockSpec((kspace, block), lambda i: (0, i)),
        ],
        out_specs=pl.BlockSpec((block, chans), lambda i: (i, 0)),
        out_shape=jax.ShapeDtypeStruct((a_dev, chans), BF16),
        scratch_shapes=[pltpu.VMEM((2, chans, kspace), BF16)],
        compiler_params=pltpu.CompilerParams(vmem_limit_bytes=48 * 1024 * 1024),
        cost_estimate=pl.CostEstimate(
            flops=4 * kspace * a_dev * chans, bytes_accessed=4 * kspace * a_dev, transcendentals=0
        ),
        name="update_rows",
    )(filt, cosine, sine)


def edges_kernel(src_ref, dst_ref, used_ref, table_ref, own_ref, send_ref, recv_ref, map_ref, out_ref, left, right, pair):
    step = pl.program_id(0)
    block = pair.shape[0]
    strip = 512

    @pl.when(step == 0)
    def _():
        def project(source, weight, target):
            def one(i, carry):
                rows = pl.ds(pl.multiple_of(i * strip, strip), strip)
                found = jnp.dot(source[rows, :], weight[...], preferred_element_type=F32)
                target[rows, :] = found.astype(BF16).astype(F32)
                return carry

            lax.fori_loop(0, source.shape[0] // strip, one, 0)

        project(table_ref, send_ref, left)
        project(own_ref, recv_ref, right)

    first = step * block
    used = used_ref[0]

    @pl.when(first < used)
    def _():
        def eight(i, carry):
            at = pl.multiple_of(i * 8, 8)
            rows = []
            for n in range(8):
                e = first + at + n
                rows.append(left[pl.ds(src_ref[e], 1), :] * right[pl.ds(dst_ref[e], 1), :])
            pair[pl.ds(at, 8), :] = jnp.concatenate(rows, axis=0)
            return carry

        lax.fori_loop(0, block // 8, eight, 0)
        orb = lax.dot_general(
            map_ref[...], pair[...].astype(BF16), (((1,), (1,)), ((), ())), preferred_element_type=F32
        )
        slots = first + lax.broadcasted_iota(jnp.int32, (1, block), 1)
        out_ref[...] = jnp.where(slots < used, orb, 0.0).astype(BF16)

    @pl.when(first >= used)
    def _():
        out_ref[...] = jnp.zeros_like(out_ref)


def edges(src, dst, used, table, own, send_w, recv_w, mapping):
    e_dev = src.shape[0]
    orbitals, chans = mapping.shape
    block = min(512, e_dev)
    whole = pl.BlockSpec(memory_space=pltpu.VMEM)
    scalars = pl.BlockSpec(memory_space=pltpu.SMEM)
    return pl.pallas_call(
        edges_kernel,
        grid=(e_dev // block,),
        in_specs=[scalars, scalars, scalars, whole, whole, whole, whole, whole],
        out_specs=pl.BlockSpec((orbitals, block), lambda i: (0, i)),
        out_shape=jax.ShapeDtypeStruct((orbitals, e_dev), BF16),
        scratch_shapes=[
            pltpu.VMEM((table.shape[0], chans), F32),
            pltpu.VMEM((own.shape[0], chans), F32),
            pltpu.VMEM((block, chans), F32),
        ],
        compiler_params=pltpu.CompilerParams(vmem_limit_bytes=48 * 1024 * 1024),
        name="edges",
    )(src, dst, used, table, own, send_w, recv_w, mapping)


def from_behind(array, axis, by):
    devices = lax.axis_size(axis)
    return lax.ppermute(array, axis, [(i, (i + by) % devices) for i in range(devices)])


def strides(devices):
    found, stride = [], 1
    for size in (2, 2):
        if devices % (stride * size) == 0 and devices > stride:
            found.append((stride, size))
            stride *= size
    if devices > stride:
        found.append((stride, devices // stride))
    return found


def shifted(array, devices, stride, size, by):
    pairs = []
    for i in range(devices):
        place = (i // stride) % size
        pairs.append((i, i + ((place + by) % size - place) * stride))
    return lax.ppermute(array, "atoms", pairs)


def scatter_sum(array, dim):
    devices = lax.axis_size("atoms")
    me = lax.axis_index("atoms")
    array = array.astype(BF16)
    for stride, size in strides(devices):
        place = (me // stride) % size
        part = array.shape[dim] // size
        total = lax.dynamic_slice_in_dim(array, place * part, part, dim).astype(F32)
        for by in range(1, size):
            away = lax.rem(place + by, size)
            piece = lax.dynamic_slice_in_dim(array, away * part, part, dim)
            total = total + shifted(piece, devices, stride, size, by).astype(F32)
        array = total.astype(BF16)
    return total


def part_start(total):
    devices = lax.axis_size("atoms")
    me = lax.axis_index("atoms")
    start = 0
    for stride, size in strides(devices):
        total = total // size
        start = start + ((me // stride) % size) * total
    return start


def gather_parts(array, dim):
    devices = lax.axis_size("atoms")
    me = lax.axis_index("atoms")
    for stride, size in reversed(strides(devices)):
        place = (me // stride) % size
        part = array.shape[dim]
        shape = list(array.shape)
        shape[dim] = part * size
        whole = lax.dynamic_update_slice_in_dim(jnp.zeros(shape, array.dtype), array, place * part, dim)
        for by in range(1, size):
            came = lax.rem(place - by + size, size)
            moved = shifted(array, devices, stride, size, by)
            whole = lax.dynamic_update_slice_in_dim(whole, moved, came * part, dim)
        array = whole
    return array


def finish_rows(feat_rows, update, gain):
    refreshed = feat_rows.astype(F32) + jax.nn.silu(update)
    scaled = refreshed * lax.rsqrt(jnp.mean(refreshed * refreshed, axis=-1, keepdims=True) + 1e-06)
    return (scaled * gain).astype(BF16)


def local(
    particle_traits,
    particle_coordinates,
    kspace_vectors,
    learned_kspace_filter,
    spatial_home,
    following_halo_lines,
    previous_halo_lines,
    sender_projection,
    receiver_projection,
    pair_channel_mapping,
    vertex_rescaling_gain,
    link_sender_line,
    link_receiver_particle,
    active_link_tally,
):
    n_atoms = lax.axis_size("atoms")
    kspace_tally = lax.axis_size("kvec")
    a_dev, chans = particle_traits.shape
    group = a_dev // n_atoms
    sub_rows = group // kspace_tally
    kspace = kspace_vectors.shape[1]
    norm_scale = 1.0 / math.sqrt(a_dev * n_atoms * kspace * kspace_tally)

    sorted_feat, sorted_coords = sort_atoms(spatial_home, particle_coordinates, particle_traits)
    k_turns = (kspace_vectors * (0.5 / math.pi)).T
    cosine, sine, sums = waves(k_turns, sorted_coords, sorted_feat)
    mine = scatter_sum(sums, 1)
    own_filter = lax.dynamic_slice_in_dim(learned_kspace_filter, part_start(kspace), kspace // n_atoms, 0)
    filt = (own_filter[None] * mine * norm_scale).astype(BF16)
    filt = gather_parts(filt, 1)
    partial = update_rows(filt, cosine, sine).reshape(n_atoms, group, chans)

    kvec_index = lax.axis_index("kvec")
    update_share = lax.dynamic_slice_in_dim(partial, kvec_index * sub_rows, sub_rows, 1).astype(F32)
    for by in range(1, kspace_tally):
        away = lax.rem(kvec_index + by, kspace_tally)
        piece = lax.dynamic_slice_in_dim(partial, away * sub_rows, sub_rows, 1)
        update_share = update_share + from_behind(piece, "kvec", by).astype(F32)
    feat_share = lax.dynamic_slice_in_dim(
        sorted_feat.reshape(n_atoms, group, chans), kvec_index * sub_rows, sub_rows, 1
    )
    node_share = finish_rows(feat_share, update_share, vertex_rescaling_gain)
    arrived = lax.all_to_all(node_share, "atoms", split_axis=0, concat_axis=0, tiled=True)
    gathered = lax.all_gather(arrived, "kvec", axis=1, tiled=True)
    partition_rows = gathered.reshape(a_dev, chans)
    from_lower = from_behind(partition_rows[following_halo_lines[0]], "atoms", 1)
    from_upper = from_behind(partition_rows[previous_halo_lines[0]], "atoms", -1)
    row_table = jnp.concatenate([partition_rows, from_lower, from_upper], axis=0)
    orbital_blocks = edges(
        link_sender_line,
        link_receiver_particle,
        active_link_tally,
        row_table,
        partition_rows,
        sender_projection,
        receiver_projection,
        pair_channel_mapping,
    )
    return (orbital_blocks, partition_rows)


def solution(mesh):
    placed = (
        P("atoms", None),
        P(None, "atoms"),
        P(None, "kvec"),
        P("kvec", None),
        P("atoms", None),
        P("atoms", None),
        P("atoms", None),
        P(),
        P(),
        P(),
        P(),
        P(("atoms", "kvec")),
        P(("atoms", "kvec")),
        P(("atoms", "kvec")),
    )
    return jax.shard_map(
        local,
        mesh=mesh,
        in_specs=placed,
        out_specs=(P(None, ("atoms", "kvec")), P("atoms", None)),
        check_vma=False,
    )
```

```python
import functools
import math

import jax
import jax.numpy as jnp
from jax import lax
from jax.experimental import pallas as pl
from jax.experimental.pallas import tpu as pltpu
from jax.sharding import PartitionSpec as P

F32 = jnp.float32
BF16 = jnp.bfloat16
ROUNDER = 12582912.0

def even_poly(function, count):
    nodes = [0.125 + 0.125 * math.cos(math.pi * (i + 0.5) / count) for i in range(count)]
    table = [function(u) for u in nodes]
    for level in range(1, count):
        for i in range(count - 1, level - 1, -1):
            table[i] = (table[i] - table[i - 1]) / (nodes[i] - nodes[i - level])
    coeffs = [table[-1]]
    for i in range(count - 2, -1, -1):
        shifted = [0.0] + coeffs
        scaled = [-nodes[i] * c for c in coeffs] + [0.0]
        coeffs = [a + b for a, b in zip(shifted, scaled)]
        coeffs[0] += table[i]
    return coeffs


SIN_POLY = even_poly(lambda u: math.sqrt(2.0) * math.sin(math.pi * math.sqrt(u)) / math.sqrt(u), 4)
COS_POLY = even_poly(lambda u: math.sqrt(2.0) * math.cos(math.pi * math.sqrt(u)), 4)


def horner(coeffs, u):
    total = coeffs[-1]
    for c in coeffs[-2::-1]:
        total = total * u + c
    return total


def cos_sin(turns):
    r = turns - ((turns + ROUNDER) - ROUNDER)
    u = r * r
    s = r * horner(SIN_POLY, u)
    c = horner(COS_POLY, u)
    return (1.0 - s * s).astype(BF16), (s * c).astype(BF16)


def sort_kernel(first, ids_ref, coords_ref, feat_ref, feat_out, coords_out):
    rows = feat_out.shape[0]
    slots = first + pl.program_id(0) * rows + lax.broadcasted_iota(jnp.int32, (rows, 1), 0)
    pick = jnp.where(slots == ids_ref[...], 1.0, 0.0).astype(BF16)
    feat_out[...] = jnp.dot(pick, feat_ref[...], preferred_element_type=F32).astype(BF16)
    x = coords_ref[...]
    high = x.astype(BF16).astype(F32)
    rest = x - high
    mid = rest.astype(BF16).astype(F32)
    low = rest - mid
    parts = jnp.concatenate([high, mid, low], axis=0).astype(BF16)
    moved = lax.dot_general(parts, pick, (((1,), (1,)), ((), ())), preferred_element_type=F32)
    coords_out[...] = moved[0:8] + moved[8:16] + moved[16:24]


def sort_atoms(places, padded, feat, first, count):
    a_dev, chans = feat.shape
    block = min(512, count)
    return pl.pallas_call(
        functools.partial(sort_kernel, first),
        grid=(count // block,),
        in_specs=[
            pl.BlockSpec((1, a_dev), lambda i: (0, 0)),
            pl.BlockSpec((8, a_dev), lambda i: (0, 0)),
            pl.BlockSpec((a_dev, chans), lambda i: (0, 0)),
        ],
        out_specs=[
            pl.BlockSpec((block, chans), lambda i: (i, 0)),
            pl.BlockSpec((8, block), lambda i: (0, i)),
        ],
        out_shape=[
            jax.ShapeDtypeStruct((count, chans), BF16),
            jax.ShapeDtypeStruct((8, count), F32),
        ],
        compiler_params=pltpu.CompilerParams(vmem_limit_bytes=48 * 1024 * 1024),
        cost_estimate=pl.CostEstimate(
            flops=4 * count * a_dev * chans, bytes_accessed=4 * count * chans, transcendentals=0
        ),
        name="sort_atoms",
    )(places, padded, feat)


def sums_kernel(chunk, k_ref, x_ref, feat_ref, sums_ref, totals):
    rows, atoms = k_ref.shape[0], x_ref.shape[1]
    totals[...] = jnp.zeros_like(totals)
    strip = 16

    def one_chunk(j, carry):
        lanes = pl.ds(pl.multiple_of(j * chunk, chunk), chunk)
        x0, x1, x2 = x_ref[0:1, lanes], x_ref[1:2, lanes], x_ref[2:3, lanes]
        coses, sines = [], []
        for top in range(0, rows, strip):
            k = k_ref[top : top + strip, :]
            turns = k[:, 0:1] * x0 + k[:, 1:2] * x1 + k[:, 2:3] * x2
            c, s = cos_sin(turns)
            coses.append(c)
            sines.append(s)
        f = feat_ref[lanes, :]
        totals[0] += jnp.dot(jnp.concatenate(coses, axis=0), f, preferred_element_type=F32)
        totals[1] += jnp.dot(jnp.concatenate(sines, axis=0), f, preferred_element_type=F32)
        return carry

    lax.fori_loop(0, atoms // chunk, one_chunk, 0)
    sums_ref[...] = totals[...].astype(BF16)


def wave_sums(k_turns, coords, feat):
    kspace = k_turns.shape[0]
    a_dev, chans = feat.shape
    block = min(256, kspace)
    return pl.pallas_call(
        functools.partial(sums_kernel, min(512, a_dev)),
        grid=(kspace // block,),
        in_specs=[
            pl.BlockSpec((block, k_turns.shape[1]), lambda i: (i, 0)),
            pl.BlockSpec((8, a_dev), lambda i: (0, 0)),
            pl.BlockSpec((a_dev, chans), lambda i: (0, 0)),
        ],
        out_specs=pl.BlockSpec((2, block, chans), lambda i: (0, i, 0)),
        out_shape=jax.ShapeDtypeStruct((2, kspace, chans), BF16),
        scratch_shapes=[pltpu.VMEM((2, block, chans), F32)],
        compiler_params=pltpu.CompilerParams(vmem_limit_bytes=48 * 1024 * 1024),
        cost_estimate=pl.CostEstimate(
            flops=10 * kspace * a_dev * chans, bytes_accessed=4 * kspace * chans, transcendentals=0
        ),
        name="wave_sums",
    )(k_turns, coords, feat)


def tables_kernel(chunk, k_ref, x_ref, cos_ref, sin_ref):
    rows, atoms = cos_ref.shape
    strip = 16

    def one_chunk(j, carry):
        lanes = pl.ds(pl.multiple_of(j * chunk, chunk), chunk)
        x0, x1, x2 = x_ref[0:1, lanes], x_ref[1:2, lanes], x_ref[2:3, lanes]
        for top in range(0, rows, strip):
            k = k_ref[top : top + strip, :]
            turns = k[:, 0:1] * x0 + k[:, 1:2] * x1 + k[:, 2:3] * x2
            c, s = cos_sin(turns)
            cos_ref[top : top + strip, lanes] = c
            sin_ref[top : top + strip, lanes] = s
        return carry

    lax.fori_loop(0, atoms // chunk, one_chunk, 0)


def wave_tables(k_turns, coords):
    kspace = k_turns.shape[0]
    atoms = coords.shape[1]
    block = min(256, kspace)
    return pl.pallas_call(
        functools.partial(tables_kernel, min(512, atoms)),
        grid=(kspace // block,),
        in_specs=[
            pl.BlockSpec((block, k_turns.shape[1]), lambda i: (i, 0)),
            pl.BlockSpec((8, atoms), lambda i: (0, 0)),
        ],
        out_specs=[pl.BlockSpec((block, atoms), lambda i: (i, 0))] * 2,
        out_shape=[jax.ShapeDtypeStruct((kspace, atoms), BF16)] * 2,
        compiler_params=pltpu.CompilerParams(vmem_limit_bytes=48 * 1024 * 1024),
        cost_estimate=pl.CostEstimate(
            flops=2000 * kspace * atoms, bytes_accessed=4 * kspace * atoms, transcendentals=0
        ),
        name="wave_tables",
    )(k_turns, coords)


def update_kernel(parts, *refs):
    filt_refs, refs = refs[:parts], refs[parts:]
    table_refs, (out_ref, turned) = refs[: 2 * parts], refs[2 * parts :]
    length = filt_refs[0].shape[1]

    @pl.when(pl.program_id(0) == 0)
    def _():
        for n, filt_ref in enumerate(filt_refs):
            for kind in range(2):
                turned[2 * n + kind] = filt_ref[kind].astype(F32).T.astype(BF16)

    total = jnp.dot(turned[0], table_refs[0][...], preferred_element_type=F32)
    for n in range(1, 2 * parts):
        total = total + jnp.dot(turned[n], table_refs[n][...], preferred_element_type=F32)
    out_ref[...] = total.T.astype(BF16)


def update_rows(filts, tables):
    length, atoms = tables[0][0].shape
    chans = filts[0].shape[2]
    block = min(512, atoms)
    flat = [table for pair in tables for table in pair]
    return pl.pallas_call(
        functools.partial(update_kernel, len(filts)),
        grid=(atoms // block,),
        in_specs=[pl.BlockSpec(filt.shape, lambda i: (0, 0, 0)) for filt in filts]
        + [pl.BlockSpec((length, block), lambda i: (0, i)) for _ in flat],
        out_specs=pl.BlockSpec((block, chans), lambda i: (i, 0)),
        out_shape=jax.ShapeDtypeStruct((atoms, chans), BF16),
        scratch_shapes=[pltpu.VMEM((len(flat), chans, length), BF16)],
        compiler_params=pltpu.CompilerParams(vmem_limit_bytes=48 * 1024 * 1024),
        cost_estimate=pl.CostEstimate(
            flops=2 * len(flat) * length * atoms * chans,
            bytes_accessed=2 * len(flat) * length * atoms,
            transcendentals=0,
        ),
        name="update_rows",
    )(*filts, *flat)


def edges_kernel(src_ref, dst_ref, used_ref, table_ref, own_ref, send_ref, recv_ref, map_ref, out_ref, left, right, pair):
    step = pl.program_id(0)
    block = pair.shape[0]
    strip = 512

    @pl.when(step == 0)
    def _():
        def project(source, weight, target):
            def one(i, carry):
                rows = pl.ds(pl.multiple_of(i * strip, strip), strip)
                found = jnp.dot(source[rows, :], weight[...], preferred_element_type=F32)
                target[rows, :] = found.astype(BF16).astype(F32)
                return carry

            lax.fori_loop(0, source.shape[0] // strip, one, 0)

        project(table_ref, send_ref, left)
        project(own_ref, recv_ref, right)

    first = step * block
    used = used_ref[0]

    @pl.when(first < used)
    def _():
        def eight(i, carry):
            at = pl.multiple_of(i * 8, 8)
            rows = []
            for n in range(8):
                e = first + at + n
                rows.append(left[pl.ds(src_ref[e], 1), :] * right[pl.ds(dst_ref[e], 1), :])
            pair[pl.ds(at, 8), :] = jnp.concatenate(rows, axis=0)
            return carry

        lax.fori_loop(0, block // 8, eight, 0)
        orb = lax.dot_general(
            map_ref[...], pair[...].astype(BF16), (((1,), (1,)), ((), ())), preferred_element_type=F32
        )
        slots = first + lax.broadcasted_iota(jnp.int32, (1, block), 1)
        out_ref[...] = jnp.where(slots < used, orb, 0.0).astype(BF16)

    @pl.when(first >= used)
    def _():
        out_ref[...] = jnp.zeros_like(out_ref)


def edges(src, dst, used, table, own, send_w, recv_w, mapping):
    e_dev = src.shape[0]
    orbitals, chans = mapping.shape
    block = min(512, e_dev)
    whole = pl.BlockSpec(memory_space=pltpu.VMEM)
    scalars = pl.BlockSpec(memory_space=pltpu.SMEM)
    return pl.pallas_call(
        edges_kernel,
        grid=(e_dev // block,),
        in_specs=[scalars, scalars, scalars, whole, whole, whole, whole, whole],
        out_specs=pl.BlockSpec((orbitals, block), lambda i: (0, i)),
        out_shape=jax.ShapeDtypeStruct((orbitals, e_dev), BF16),
        scratch_shapes=[
            pltpu.VMEM((table.shape[0], chans), F32),
            pltpu.VMEM((own.shape[0], chans), F32),
            pltpu.VMEM((block, chans), F32),
        ],
        compiler_params=pltpu.CompilerParams(vmem_limit_bytes=48 * 1024 * 1024),
        name="edges",
    )(src, dst, used, table, own, send_w, recv_w, mapping)


def from_behind(array, axis, by):
    devices = lax.axis_size(axis)
    return lax.ppermute(array, axis, [(i, (i + by) % devices) for i in range(devices)])


def strides(devices):
    found, stride = [], 1
    for size in (2, 2):
        if devices % (stride * size) == 0 and devices > stride:
            found.append((stride, size))
            stride *= size
    if devices > stride:
        found.append((stride, devices // stride))
    return found


def shifted(array, devices, stride, size, by):
    pairs = []
    for i in range(devices):
        place = (i // stride) % size
        pairs.append((i, i + ((place + by) % size - place) * stride))
    return lax.ppermute(array, "atoms", pairs)


def sum_stage(array, dim, stride, size):
    devices = lax.axis_size("atoms")
    place = (lax.axis_index("atoms") // stride) % size
    part = array.shape[dim] // size
    total = lax.dynamic_slice_in_dim(array, place * part, part, dim).astype(F32)
    for by in range(1, size):
        away = lax.rem(place + by, size)
        piece = lax.dynamic_slice_in_dim(array, away * part, part, dim)
        total = total + shifted(piece, devices, stride, size, by).astype(F32)
    return total


def part_start(total):
    devices = lax.axis_size("atoms")
    me = lax.axis_index("atoms")
    start = 0
    for stride, size in strides(devices):
        total = total // size
        start = start + ((me // stride) % size) * total
    return start


def gather_stage(array, dim, stride, size):
    devices = lax.axis_size("atoms")
    place = (lax.axis_index("atoms") // stride) % size
    part = array.shape[dim]
    shape = list(array.shape)
    shape[dim] = part * size
    whole = lax.dynamic_update_slice_in_dim(jnp.zeros(shape, array.dtype), array, place * part, dim)
    for by in range(1, size):
        came = lax.rem(place - by + size, size)
        moved = shifted(array, devices, stride, size, by)
        whole = lax.dynamic_update_slice_in_dim(whole, moved, came * part, dim)
    return whole


def structure_stages(own_filter, norm_scale):
    factors = strides(lax.axis_size("atoms"))
    steps = []
    for n, (stride, size) in enumerate(factors):
        def add(array, stride=stride, size=size, last=n == len(factors) - 1):
            total = sum_stage(array, 1, stride, size)
            if last:
                total = own_filter[None] * total * norm_scale
            return total.astype(BF16)

        steps.append(add)
    for stride, size in reversed(factors):
        steps.append(lambda array, stride=stride, size=size: gather_stage(array, 1, stride, size))
    return steps


def finish_rows(feat_rows, update, gain):
    refreshed = feat_rows.astype(F32) + jax.nn.silu(update)
    scaled = refreshed * lax.rsqrt(jnp.mean(refreshed * refreshed, axis=-1, keepdims=True) + 1e-06)
    return (scaled * gain).astype(BF16)


def local(
    particle_traits,
    particle_coordinates,
    kspace_vectors,
    learned_kspace_filter,
    spatial_home,
    following_halo_lines,
    previous_halo_lines,
    sender_projection,
    receiver_projection,
    pair_channel_mapping,
    vertex_rescaling_gain,
    link_sender_line,
    link_receiver_particle,
    active_link_tally,
):
    n_atoms = lax.axis_size("atoms")
    kspace_tally = lax.axis_size("kvec")
    a_dev, chans = particle_traits.shape
    group = a_dev // n_atoms
    sub_rows = group // kspace_tally
    kspace = kspace_vectors.shape[1]
    norm_scale = 1.0 / math.sqrt(a_dev * n_atoms * kspace * kspace_tally)

    pieces = 2
    padded = jnp.concatenate([particle_coordinates, jnp.zeros((8 - particle_coordinates.shape[0], a_dev), F32)], axis=0)
    k_turns = (kspace_vectors * (0.5 / math.pi)).T

    share = sub_rows // pieces
    count = a_dev // pieces
    within = spatial_home % sub_rows
    places = (within // share) * count + (spatial_home // sub_rows) * share + within % share
    kvec_index = lax.axis_index("kvec")

    k_part = kspace // pieces
    quarter = k_part // 2
    made = {}

    def sums_of(key, first):
        def work(k, x, f):
            made[key] = wave_sums(lax.slice_in_dim(k, first, first + quarter), x, f)
            return made[key]

        return work

    def sort_of(n):
        def work(k, x, f):
            made["sort", n] = sort_atoms(places, x, f, n * count, count)
            return made["sort", n]

        return work

    def tables_of(n, half):
        def work(k, x, f):
            k_half = lax.slice_in_dim(k, half * k_part, (half + 1) * k_part)
            made["tables", n, half] = wave_tables(k_half, made["sort", n][1])
            return made["tables", n, half]

        return work

    works = [
        sums_of("c", k_part),
        sums_of("d", k_part + quarter),
        sort_of(0),
        tables_of(0, 0),
        tables_of(0, 1),
        sort_of(1),
        tables_of(1, 0),
        tables_of(1, 1),
    ]
    steps = []
    for n in range(pieces):
        own_filter = lax.dynamic_slice_in_dim(
            learned_kspace_filter, n * k_part + part_start(k_part), k_part // n_atoms, 0
        )
        steps.append(structure_stages(own_filter, norm_scale))
    lag = 2
    inputs = (k_turns, padded, particle_traits)
    states = [wave_sums(lax.slice_in_dim(k_turns, 0, k_part), padded, particle_traits), None]
    for turn in range(max(len(works), lag + len(steps[1]))):
        if turn == lag:
            states[1] = jnp.concatenate([made["c"], made["d"]], axis=1)
        states, inputs = lax.optimization_barrier((states, inputs))
        done = works[turn](*inputs) if turn < len(works) else None
        for n in range(pieces):
            step = turn - n * lag
            if 0 <= step < len(steps[n]):
                states[n] = steps[n][step](states[n])
        states, inputs, done = lax.optimization_barrier((states, inputs, done))
        if turn < len(works):
            made[list(made)[-1]] = done
    filts = states

    updates, feats = [], []
    for n in range(pieces):
        tables = [made["tables", n, half] for half in range(2)]
        partial = update_rows(filts, tables).reshape(n_atoms, kspace_tally, share, chans)
        update = [lax.dynamic_index_in_dim(partial, kvec_index, 1, False)]
        for by in range(1, kspace_tally):
            away = lax.rem(kvec_index + by, kspace_tally)
            piece = lax.dynamic_index_in_dim(partial, away, 1, False)
            update.append(from_behind(piece, "kvec", by))
        updates.append(update)
        feat = made["sort", n][0].reshape(n_atoms, kspace_tally, share, chans)
        feats.append(lax.dynamic_index_in_dim(feat, kvec_index, 1, False))
    partition_rows = jnp.zeros((n_atoms, kspace_tally, pieces, share, chans), BF16)
    arrived = None
    for n in range(pieces):
        update = updates[n]
        if n:
            update, arrived = lax.optimization_barrier((update, arrived))
        update = sum(term.astype(F32) for term in update)
        node = finish_rows(feats[n], update, vertex_rescaling_gain)
        arrived = lax.all_to_all(node, "atoms", split_axis=0, concat_axis=0, tiled=True)
        for by in range(kspace_tally):
            came = lax.rem(kvec_index - by + kspace_tally, kspace_tally)
            moved = arrived if by == 0 else from_behind(arrived, "kvec", by)
            partition_rows = lax.dynamic_update_slice(
                partition_rows, moved[:, None, None], (0, came, n, 0, 0)
            )
    partition_rows = partition_rows.reshape(a_dev, chans)
    from_lower = from_behind(partition_rows[following_halo_lines[0]], "atoms", 1)
    from_upper = from_behind(partition_rows[previous_halo_lines[0]], "atoms", -1)
    row_table = jnp.concatenate([partition_rows, from_lower, from_upper], axis=0)
    orbital_blocks = edges(
        link_sender_line,
        link_receiver_particle,
        active_link_tally,
        row_table,
        partition_rows,
        sender_projection,
        receiver_projection,
        pair_channel_mapping,
    )
    return (orbital_blocks, partition_rows)


def solution(mesh):
    placed = (
        P("atoms", None),
        P(None, "atoms"),
        P(None, "kvec"),
        P("kvec", None),
        P("atoms", None),
        P("atoms", None),
        P("atoms", None),
        P(),
        P(),
        P(),
        P(),
        P(("atoms", "kvec")),
        P(("atoms", "kvec")),
        P(("atoms", "kvec")),
    )
    return jax.shard_map(
        local,
        mesh=mesh,
        in_specs=placed,
        out_specs=(P(None, ("atoms", "kvec")), P("atoms", None)),
        check_vma=False,
    )
```

```python
import functools
import math

import jax
import jax.numpy as jnp
from jax import lax
from jax.experimental import pallas as pl
from jax.experimental.pallas import tpu as pltpu
from jax.sharding import PartitionSpec as P

F32 = jnp.float32
BF16 = jnp.bfloat16
ROUNDER = 12582912.0

def even_poly(function, count):
    nodes = [0.125 + 0.125 * math.cos(math.pi * (i + 0.5) / count) for i in range(count)]
    table = [function(u) for u in nodes]
    for level in range(1, count):
        for i in range(count - 1, level - 1, -1):
            table[i] = (table[i] - table[i - 1]) / (nodes[i] - nodes[i - level])
    coeffs = [table[-1]]
    for i in range(count - 2, -1, -1):
        shifted = [0.0] + coeffs
        scaled = [-nodes[i] * c for c in coeffs] + [0.0]
        coeffs = [a + b for a, b in zip(shifted, scaled)]
        coeffs[0] += table[i]
    return coeffs


SIN_POLY = even_poly(lambda u: math.sqrt(2.0) * math.sin(math.pi * math.sqrt(u)) / math.sqrt(u), 4)
COS_POLY = even_poly(lambda u: math.sqrt(2.0) * math.cos(math.pi * math.sqrt(u)), 4)


def horner(coeffs, u):
    total = coeffs[-1]
    for c in coeffs[-2::-1]:
        total = total * u + c
    return total


def cos_sin(turns):
    r = turns - ((turns + ROUNDER) - ROUNDER)
    u = r * r
    s = r * horner(SIN_POLY, u)
    c = horner(COS_POLY, u)
    return (1.0 - s * s).astype(BF16), (s * c).astype(BF16)


def sort_kernel(first, ids_ref, coords_ref, feat_ref, feat_out, coords_out):
    rows = feat_out.shape[0]
    slots = first + pl.program_id(0) * rows + lax.broadcasted_iota(jnp.int32, (rows, 1), 0)
    pick = jnp.where(slots == ids_ref[...], 1.0, 0.0).astype(BF16)
    feat_out[...] = jnp.dot(pick, feat_ref[...], preferred_element_type=F32).astype(BF16)
    x = coords_ref[...]
    high = x.astype(BF16).astype(F32)
    rest = x - high
    mid = rest.astype(BF16).astype(F32)
    low = rest - mid
    parts = jnp.concatenate([high, mid, low], axis=0).astype(BF16)
    moved = lax.dot_general(parts, pick, (((1,), (1,)), ((), ())), preferred_element_type=F32)
    coords_out[...] = moved[0:8] + moved[8:16] + moved[16:24]


def sort_atoms(places, padded, feat, first, count):
    a_dev, chans = feat.shape
    block = min(512, count)
    return pl.pallas_call(
        functools.partial(sort_kernel, first),
        grid=(count // block,),
        in_specs=[
            pl.BlockSpec((1, a_dev), lambda i: (0, 0)),
            pl.BlockSpec((8, a_dev), lambda i: (0, 0)),
            pl.BlockSpec((a_dev, chans), lambda i: (0, 0)),
        ],
        out_specs=[
            pl.BlockSpec((block, chans), lambda i: (i, 0)),
            pl.BlockSpec((8, block), lambda i: (0, i)),
        ],
        out_shape=[
            jax.ShapeDtypeStruct((count, chans), BF16),
            jax.ShapeDtypeStruct((8, count), F32),
        ],
        compiler_params=pltpu.CompilerParams(vmem_limit_bytes=48 * 1024 * 1024),
        cost_estimate=pl.CostEstimate(
            flops=4 * count * a_dev * chans, bytes_accessed=4 * count * chans, transcendentals=0
        ),
        name="sort_atoms",
    )(places, padded, feat)


def sums_kernel(chunk, k_ref, x_ref, feat_ref, sums_ref, cos_ref, sin_ref, totals):
    rows, atoms = k_ref.shape[0], x_ref.shape[1]
    totals[...] = jnp.zeros_like(totals)
    strip = 16

    def one_chunk(j, carry):
        lanes = pl.ds(pl.multiple_of(j * chunk, chunk), chunk)
        x0, x1, x2 = x_ref[0:1, lanes], x_ref[1:2, lanes], x_ref[2:3, lanes]
        coses, sines = [], []
        for top in range(0, rows, strip):
            k = k_ref[top : top + strip, :]
            turns = k[:, 0:1] * x0 + k[:, 1:2] * x1 + k[:, 2:3] * x2
            c, s = cos_sin(turns)
            coses.append(c)
            sines.append(s)
        c = jnp.concatenate(coses, axis=0)
        s = jnp.concatenate(sines, axis=0)
        cos_ref[:, lanes] = c
        sin_ref[:, lanes] = s
        f = feat_ref[lanes, :]
        totals[0] += jnp.dot(c, f, preferred_element_type=F32)
        totals[1] += jnp.dot(s, f, preferred_element_type=F32)
        return carry

    lax.fori_loop(0, atoms // chunk, one_chunk, 0)
    sums_ref[...] = totals[...].astype(BF16)


def wave_sums(k_turns, coords, feat):
    kspace = k_turns.shape[0]
    a_dev, chans = feat.shape
    block = min(256, kspace)
    return pl.pallas_call(
        functools.partial(sums_kernel, min(512, a_dev)),
        grid=(kspace // block,),
        in_specs=[
            pl.BlockSpec((block, k_turns.shape[1]), lambda i: (i, 0)),
            pl.BlockSpec((8, a_dev), lambda i: (0, 0)),
            pl.BlockSpec((a_dev, chans), lambda i: (0, 0)),
        ],
        out_specs=[pl.BlockSpec((2, block, chans), lambda i: (0, i, 0))]
        + [pl.BlockSpec((block, a_dev), lambda i: (i, 0))] * 2,
        out_shape=[jax.ShapeDtypeStruct((2, kspace, chans), BF16)]
        + [jax.ShapeDtypeStruct((kspace, a_dev), BF16)] * 2,
        scratch_shapes=[pltpu.VMEM((2, block, chans), F32)],
        compiler_params=pltpu.CompilerParams(vmem_limit_bytes=48 * 1024 * 1024),
        cost_estimate=pl.CostEstimate(
            flops=10 * kspace * a_dev * chans, bytes_accessed=4 * kspace * chans, transcendentals=0
        ),
        name="wave_sums",
    )(k_turns, coords, feat)


def update_kernel(parts, *refs):
    filt_refs, refs = refs[:parts], refs[parts:]
    table_refs, (out_ref, turned) = refs[: 2 * parts], refs[2 * parts :]
    length = filt_refs[0].shape[1]

    @pl.when(pl.program_id(0) == 0)
    def _():
        for n, filt_ref in enumerate(filt_refs):
            for kind in range(2):
                turned[2 * n + kind] = filt_ref[kind].astype(F32).T.astype(BF16)

    total = jnp.dot(turned[0], table_refs[0][...], preferred_element_type=F32)
    for n in range(1, 2 * parts):
        total = total + jnp.dot(turned[n], table_refs[n][...], preferred_element_type=F32)
    out_ref[...] = total.T.astype(BF16)


def update_rows(filts, tables):
    length, atoms = tables[0][0].shape
    chans = filts[0].shape[2]
    block = min(512, atoms)
    flat = [table for pair in tables for table in pair]
    return pl.pallas_call(
        functools.partial(update_kernel, len(filts)),
        grid=(atoms // block,),
        in_specs=[pl.BlockSpec(filt.shape, lambda i: (0, 0, 0)) for filt in filts]
        + [pl.BlockSpec((length, block), lambda i: (0, i)) for _ in flat],
        out_specs=pl.BlockSpec((block, chans), lambda i: (i, 0)),
        out_shape=jax.ShapeDtypeStruct((atoms, chans), BF16),
        scratch_shapes=[pltpu.VMEM((len(flat), chans, length), BF16)],
        compiler_params=pltpu.CompilerParams(vmem_limit_bytes=48 * 1024 * 1024),
        cost_estimate=pl.CostEstimate(
            flops=2 * len(flat) * length * atoms * chans,
            bytes_accessed=2 * len(flat) * length * atoms,
            transcendentals=0,
        ),
        name="update_rows",
    )(*filts, *flat)


def edges_kernel(src_ref, dst_ref, used_ref, table_ref, own_ref, send_ref, recv_ref, map_ref, out_ref, left, right, pair):
    step = pl.program_id(0)
    block = pair.shape[0]
    strip = 512

    @pl.when(step == 0)
    def _():
        def project(source, weight, target):
            def one(i, carry):
                rows = pl.ds(pl.multiple_of(i * strip, strip), strip)
                found = jnp.dot(source[rows, :], weight[...], preferred_element_type=F32)
                target[rows, :] = found.astype(BF16).astype(F32)
                return carry

            lax.fori_loop(0, source.shape[0] // strip, one, 0)

        project(table_ref, send_ref, left)
        project(own_ref, recv_ref, right)

    first = step * block
    used = used_ref[0]

    @pl.when(first < used)
    def _():
        def eight(i, carry):
            at = pl.multiple_of(i * 8, 8)
            rows = []
            for n in range(8):
                e = first + at + n
                rows.append(left[pl.ds(src_ref[e], 1), :] * right[pl.ds(dst_ref[e], 1), :])
            pair[pl.ds(at, 8), :] = jnp.concatenate(rows, axis=0)
            return carry

        lax.fori_loop(0, block // 8, eight, 0)
        orb = lax.dot_general(
            map_ref[...], pair[...].astype(BF16), (((1,), (1,)), ((), ())), preferred_element_type=F32
        )
        slots = first + lax.broadcasted_iota(jnp.int32, (1, block), 1)
        out_ref[...] = jnp.where(slots < used, orb, 0.0).astype(BF16)

    @pl.when(first >= used)
    def _():
        out_ref[...] = jnp.zeros_like(out_ref)


def edges(src, dst, used, table, own, send_w, recv_w, mapping):
    e_dev = src.shape[0]
    orbitals, chans = mapping.shape
    block = min(512, e_dev)
    whole = pl.BlockSpec(memory_space=pltpu.VMEM)
    scalars = pl.BlockSpec(memory_space=pltpu.SMEM)
    return pl.pallas_call(
        edges_kernel,
        grid=(e_dev // block,),
        in_specs=[scalars, scalars, scalars, whole, whole, whole, whole, whole],
        out_specs=pl.BlockSpec((orbitals, block), lambda i: (0, i)),
        out_shape=jax.ShapeDtypeStruct((orbitals, e_dev), BF16),
        scratch_shapes=[
            pltpu.VMEM((table.shape[0], chans), F32),
            pltpu.VMEM((own.shape[0], chans), F32),
            pltpu.VMEM((block, chans), F32),
        ],
        compiler_params=pltpu.CompilerParams(vmem_limit_bytes=48 * 1024 * 1024),
        name="edges",
    )(src, dst, used, table, own, send_w, recv_w, mapping)


def from_behind(array, axis, by):
    devices = lax.axis_size(axis)
    return lax.ppermute(array, axis, [(i, (i + by) % devices) for i in range(devices)])


def strides(devices):
    found, stride = [], 1
    for size in (2, 2):
        if devices % (stride * size) == 0 and devices > stride:
            found.append((stride, size))
            stride *= size
    if devices > stride:
        found.append((stride, devices // stride))
    return found


def shifted(array, devices, stride, size, by):
    pairs = []
    for i in range(devices):
        place = (i // stride) % size
        pairs.append((i, i + ((place + by) % size - place) * stride))
    return lax.ppermute(array, "atoms", pairs)


def sum_stage(array, dim, stride, size):
    devices = lax.axis_size("atoms")
    place = (lax.axis_index("atoms") // stride) % size
    part = array.shape[dim] // size
    total = lax.dynamic_slice_in_dim(array, place * part, part, dim).astype(F32)
    for by in range(1, size):
        away = lax.rem(place + by, size)
        piece = lax.dynamic_slice_in_dim(array, away * part, part, dim)
        total = total + shifted(piece, devices, stride, size, by).astype(F32)
    return total


def part_start(total):
    devices = lax.axis_size("atoms")
    me = lax.axis_index("atoms")
    start = 0
    for stride, size in strides(devices):
        total = total // size
        start = start + ((me // stride) % size) * total
    return start


def gather_stage(array, dim, stride, size):
    devices = lax.axis_size("atoms")
    place = (lax.axis_index("atoms") // stride) % size
    part = array.shape[dim]
    shape = list(array.shape)
    shape[dim] = part * size
    whole = lax.dynamic_update_slice_in_dim(jnp.zeros(shape, array.dtype), array, place * part, dim)
    for by in range(1, size):
        came = lax.rem(place - by + size, size)
        moved = shifted(array, devices, stride, size, by)
        whole = lax.dynamic_update_slice_in_dim(whole, moved, came * part, dim)
    return whole


def structure_stages(own_filter, norm_scale):
    factors = strides(lax.axis_size("atoms"))
    steps = []
    for n, (stride, size) in enumerate(factors):
        def add(array, stride=stride, size=size, last=n == len(factors) - 1):
            total = sum_stage(array, 1, stride, size)
            if last:
                total = own_filter[None] * total * norm_scale
            return total.astype(BF16)

        steps.append(add)
    for stride, size in reversed(factors):
        steps.append(lambda array, stride=stride, size=size: gather_stage(array, 1, stride, size))
    return steps


def finish_rows(feat_rows, update, gain):
    refreshed = feat_rows.astype(F32) + jax.nn.silu(update)
    scaled = refreshed * lax.rsqrt(jnp.mean(refreshed * refreshed, axis=-1, keepdims=True) + 1e-06)
    return (scaled * gain).astype(BF16)


def local(
    particle_traits,
    particle_coordinates,
    kspace_vectors,
    learned_kspace_filter,
    spatial_home,
    following_halo_lines,
    previous_halo_lines,
    sender_projection,
    receiver_projection,
    pair_channel_mapping,
    vertex_rescaling_gain,
    link_sender_line,
    link_receiver_particle,
    active_link_tally,
):
    n_atoms = lax.axis_size("atoms")
    kspace_tally = lax.axis_size("kvec")
    a_dev, chans = particle_traits.shape
    group = a_dev // n_atoms
    sub_rows = group // kspace_tally
    kspace = kspace_vectors.shape[1]
    norm_scale = 1.0 / math.sqrt(a_dev * n_atoms * kspace * kspace_tally)

    pieces = 2
    padded = jnp.concatenate([particle_coordinates, jnp.zeros((8 - particle_coordinates.shape[0], a_dev), F32)], axis=0)
    k_turns = (kspace_vectors * (0.5 / math.pi)).T

    share = sub_rows // pieces
    count = a_dev // pieces
    within = spatial_home % sub_rows
    places = (within // share) * count + (spatial_home // sub_rows) * share + within % share
    kvec_index = lax.axis_index("kvec")

    k_part = kspace // pieces
    made = {}

    def waves_of(half, n, k):
        k_half = lax.slice_in_dim(k, half * k_part, (half + 1) * k_part)
        made[half, n] = wave_sums(k_half, placed[n][1], placed[n][0])

    def sums_of(half):
        return sum(made[half, n][0].astype(F32) for n in range(pieces)).astype(BF16)

    placed = [sort_atoms(places, padded, particle_traits, n * count, count) for n in range(pieces)]
    steps = []
    for half in range(2):
        own_filter = lax.dynamic_slice_in_dim(
            learned_kspace_filter, half * k_part + part_start(k_part), k_part // n_atoms, 0
        )
        steps.append(structure_stages(own_filter, norm_scale))
    for n in range(pieces):
        waves_of(0, n, k_turns)
    state = sums_of(0)
    for n in range(pieces):
        state, k_turns = lax.optimization_barrier((state, k_turns))
        waves_of(1, n, k_turns)
        state = steps[0][n](state)
        state, k_turns, made[1, n] = lax.optimization_barrier((state, k_turns, made[1, n]))
    last = sums_of(1)
    for turn in range(len(steps[1])):
        last = steps[1][turn](last)
        if turn + pieces < len(steps[0]):
            state = steps[0][turn + pieces](state)
    filts = [state, last]

    updates, feats = [], []
    for n in range(pieces):
        partial = update_rows(filts, [made[half, n][1:] for half in range(2)])
        partial = partial.reshape(n_atoms, kspace_tally, share, chans)
        update = [lax.dynamic_index_in_dim(partial, kvec_index, 1, False)]
        for by in range(1, kspace_tally):
            away = lax.rem(kvec_index + by, kspace_tally)
            piece = lax.dynamic_index_in_dim(partial, away, 1, False)
            update.append(from_behind(piece, "kvec", by))
        updates.append(update)
        feat = placed[n][0].reshape(n_atoms, kspace_tally, share, chans)
        feats.append(lax.dynamic_index_in_dim(feat, kvec_index, 1, False))
    for n in range(pieces - 1):
        updates[n], updates[n + 1][0] = lax.optimization_barrier((updates[n], updates[n + 1][0]))
    partition_rows = jnp.zeros((n_atoms, kspace_tally, pieces, share, chans), BF16)
    arrived = None
    for n in range(pieces):
        update = updates[n]
        if n:
            update, arrived = lax.optimization_barrier((update, arrived))
        update = sum(term.astype(F32) for term in update)
        node = finish_rows(feats[n], update, vertex_rescaling_gain)
        arrived = lax.all_to_all(node, "atoms", split_axis=0, concat_axis=0, tiled=True)
        for by in range(kspace_tally):
            came = lax.rem(kvec_index - by + kspace_tally, kspace_tally)
            moved = arrived if by == 0 else from_behind(arrived, "kvec", by)
            partition_rows = lax.dynamic_update_slice(
                partition_rows, moved[:, None, None], (0, came, n, 0, 0)
            )
    partition_rows = partition_rows.reshape(a_dev, chans)
    from_lower = from_behind(partition_rows[following_halo_lines[0]], "atoms", 1)
    from_upper = from_behind(partition_rows[previous_halo_lines[0]], "atoms", -1)
    row_table = jnp.concatenate([partition_rows, from_lower, from_upper], axis=0)
    orbital_blocks = edges(
        link_sender_line,
        link_receiver_particle,
        active_link_tally,
        row_table,
        partition_rows,
        sender_projection,
        receiver_projection,
        pair_channel_mapping,
    )
    return (orbital_blocks, partition_rows)


def solution(mesh):
    placed = (
        P("atoms", None),
        P(None, "atoms"),
        P(None, "kvec"),
        P("kvec", None),
        P("atoms", None),
        P("atoms", None),
        P("atoms", None),
        P(),
        P(),
        P(),
        P(),
        P(("atoms", "kvec")),
        P(("atoms", "kvec")),
        P(("atoms", "kvec")),
    )
    return jax.shard_map(
        local,
        mesh=mesh,
        in_specs=placed,
        out_specs=(P(None, ("atoms", "kvec")), P("atoms", None)),
        check_vma=False,
    )
```

```python
import functools
import math

import jax
import jax.numpy as jnp
from jax import lax
from jax.experimental import pallas as pl
from jax.experimental.pallas import tpu as pltpu
from jax.sharding import PartitionSpec as P

F32 = jnp.float32
BF16 = jnp.bfloat16
ROUNDER = 12582912.0

def even_poly(function, count):
    nodes = [0.125 + 0.125 * math.cos(math.pi * (i + 0.5) / count) for i in range(count)]
    table = [function(u) for u in nodes]
    for level in range(1, count):
        for i in range(count - 1, level - 1, -1):
            table[i] = (table[i] - table[i - 1]) / (nodes[i] - nodes[i - level])
    coeffs = [table[-1]]
    for i in range(count - 2, -1, -1):
        shifted = [0.0] + coeffs
        scaled = [-nodes[i] * c for c in coeffs] + [0.0]
        coeffs = [a + b for a, b in zip(shifted, scaled)]
        coeffs[0] += table[i]
    return coeffs


SIN_POLY = even_poly(lambda u: math.sqrt(2.0) * math.sin(math.pi * math.sqrt(u)) / math.sqrt(u), 4)
COS_POLY = even_poly(lambda u: math.sqrt(2.0) * math.cos(math.pi * math.sqrt(u)), 4)


def horner(coeffs, u):
    total = coeffs[-1]
    for c in coeffs[-2::-1]:
        total = total * u + c
    return total


def cos_sin(turns):
    r = turns - ((turns + ROUNDER) - ROUNDER)
    u = r * r
    s = r * horner(SIN_POLY, u)
    c = horner(COS_POLY, u)
    return (1.0 - s * s).astype(BF16), (s * c).astype(BF16)


def sort_kernel(first, ids_ref, coords_ref, feat_ref, feat_out, coords_out):
    rows = feat_out.shape[0]
    slots = first + pl.program_id(0) * rows + lax.broadcasted_iota(jnp.int32, (rows, 1), 0)
    pick = jnp.where(slots == ids_ref[...], 1.0, 0.0).astype(BF16)
    feat_out[...] = jnp.dot(pick, feat_ref[...], preferred_element_type=F32).astype(BF16)
    x = coords_ref[...]
    high = x.astype(BF16).astype(F32)
    rest = x - high
    mid = rest.astype(BF16).astype(F32)
    low = rest - mid
    parts = jnp.concatenate([high, mid, low], axis=0).astype(BF16)
    moved = lax.dot_general(parts, pick, (((1,), (1,)), ((), ())), preferred_element_type=F32)
    coords_out[...] = moved[0:8] + moved[8:16] + moved[16:24]


def sort_atoms(places, padded, feat, first, count):
    a_dev, chans = feat.shape
    block = min(512, count)
    return pl.pallas_call(
        functools.partial(sort_kernel, first),
        grid=(count // block,),
        in_specs=[
            pl.BlockSpec((1, a_dev), lambda i: (0, 0)),
            pl.BlockSpec((8, a_dev), lambda i: (0, 0)),
            pl.BlockSpec((a_dev, chans), lambda i: (0, 0)),
        ],
        out_specs=[
            pl.BlockSpec((block, chans), lambda i: (i, 0)),
            pl.BlockSpec((8, block), lambda i: (0, i)),
        ],
        out_shape=[
            jax.ShapeDtypeStruct((count, chans), BF16),
            jax.ShapeDtypeStruct((8, count), F32),
        ],
        compiler_params=pltpu.CompilerParams(vmem_limit_bytes=48 * 1024 * 1024),
        cost_estimate=pl.CostEstimate(
            flops=4 * count * a_dev * chans, bytes_accessed=4 * count * chans, transcendentals=0
        ),
        name="sort_atoms",
    )(places, padded, feat)


def sums_kernel(chunk, k_ref, x_ref, feat_ref, sums_ref, cos_ref, sin_ref, totals):
    rows, atoms = k_ref.shape[0], x_ref.shape[1]
    totals[...] = jnp.zeros_like(totals)
    strip = 16

    def one_chunk(j, carry):
        lanes = pl.ds(pl.multiple_of(j * chunk, chunk), chunk)
        x0, x1, x2 = x_ref[0:1, lanes], x_ref[1:2, lanes], x_ref[2:3, lanes]
        coses, sines = [], []
        for top in range(0, rows, strip):
            k = k_ref[top : top + strip, :]
            turns = k[:, 0:1] * x0 + k[:, 1:2] * x1 + k[:, 2:3] * x2
            c, s = cos_sin(turns)
            coses.append(c)
            sines.append(s)
        c = jnp.concatenate(coses, axis=0)
        s = jnp.concatenate(sines, axis=0)
        cos_ref[:, lanes] = c
        sin_ref[:, lanes] = s
        f = feat_ref[lanes, :]
        totals[0] += jnp.dot(c, f, preferred_element_type=F32)
        totals[1] += jnp.dot(s, f, preferred_element_type=F32)
        return carry

    lax.fori_loop(0, atoms // chunk, one_chunk, 0)
    sums_ref[...] = totals[...].astype(BF16)


def wave_sums(k_turns, coords, feat):
    kspace = k_turns.shape[0]
    a_dev, chans = feat.shape
    block = min(256, kspace)
    return pl.pallas_call(
        functools.partial(sums_kernel, min(512, a_dev)),
        grid=(kspace // block,),
        in_specs=[
            pl.BlockSpec((block, k_turns.shape[1]), lambda i: (i, 0)),
            pl.BlockSpec((8, a_dev), lambda i: (0, 0)),
            pl.BlockSpec((a_dev, chans), lambda i: (0, 0)),
        ],
        out_specs=[pl.BlockSpec((2, block, chans), lambda i: (0, i, 0))]
        + [pl.BlockSpec((block, a_dev), lambda i: (i, 0))] * 2,
        out_shape=[jax.ShapeDtypeStruct((2, kspace, chans), BF16)]
        + [jax.ShapeDtypeStruct((kspace, a_dev), BF16)] * 2,
        scratch_shapes=[pltpu.VMEM((2, block, chans), F32)],
        compiler_params=pltpu.CompilerParams(vmem_limit_bytes=48 * 1024 * 1024),
        cost_estimate=pl.CostEstimate(
            flops=10 * kspace * a_dev * chans, bytes_accessed=4 * kspace * chans, transcendentals=0
        ),
        name="wave_sums",
    )(k_turns, coords, feat)


def update_kernel(parts, *refs):
    filt_refs, refs = refs[:parts], refs[parts:]
    table_refs, (out_ref, turned) = refs[: 2 * parts], refs[2 * parts :]
    length = filt_refs[0].shape[1]

    @pl.when(pl.program_id(0) == 0)
    def _():
        for n, filt_ref in enumerate(filt_refs):
            for kind in range(2):
                turned[2 * n + kind] = filt_ref[kind].astype(F32).T.astype(BF16)

    total = jnp.dot(turned[0], table_refs[0][...], preferred_element_type=F32)
    for n in range(1, 2 * parts):
        total = total + jnp.dot(turned[n], table_refs[n][...], preferred_element_type=F32)
    out_ref[...] = total.T.astype(BF16)


def update_rows(filts, tables):
    length, atoms = tables[0][0].shape
    chans = filts[0].shape[2]
    block = min(512, atoms)
    flat = [table for pair in tables for table in pair]
    return pl.pallas_call(
        functools.partial(update_kernel, len(filts)),
        grid=(atoms // block,),
        in_specs=[pl.BlockSpec(filt.shape, lambda i: (0, 0, 0)) for filt in filts]
        + [pl.BlockSpec((length, block), lambda i: (0, i)) for _ in flat],
        out_specs=pl.BlockSpec((block, chans), lambda i: (i, 0)),
        out_shape=jax.ShapeDtypeStruct((atoms, chans), BF16),
        scratch_shapes=[pltpu.VMEM((len(flat), chans, length), BF16)],
        compiler_params=pltpu.CompilerParams(vmem_limit_bytes=48 * 1024 * 1024),
        cost_estimate=pl.CostEstimate(
            flops=2 * len(flat) * length * atoms * chans,
            bytes_accessed=2 * len(flat) * length * atoms,
            transcendentals=0,
        ),
        name="update_rows",
    )(*filts, *flat)


def edges_kernel(src_ref, dst_ref, used_ref, table_ref, own_ref, send_ref, recv_ref, map_ref, out_ref, left, right, pair):
    step = pl.program_id(0)
    block = pair.shape[0]
    strip = 512

    @pl.when(step == 0)
    def _():
        def project(source, weight, target):
            def one(i, carry):
                rows = pl.ds(pl.multiple_of(i * strip, strip), strip)
                found = jnp.dot(source[rows, :], weight[...], preferred_element_type=F32)
                target[rows, :] = found.astype(BF16).astype(F32)
                return carry

            lax.fori_loop(0, source.shape[0] // strip, one, 0)

        project(table_ref, send_ref, left)
        project(own_ref, recv_ref, right)

    first = step * block
    used = used_ref[0]

    @pl.when(first < used)
    def _():
        def eight(i, carry):
            at = pl.multiple_of(i * 8, 8)
            rows = []
            for n in range(8):
                e = first + at + n
                rows.append(left[pl.ds(src_ref[e], 1), :] * right[pl.ds(dst_ref[e], 1), :])
            pair[pl.ds(at, 8), :] = jnp.concatenate(rows, axis=0)
            return carry

        lax.fori_loop(0, block // 8, eight, 0)
        orb = lax.dot_general(
            map_ref[...], pair[...].astype(BF16), (((1,), (1,)), ((), ())), preferred_element_type=F32
        )
        slots = first + lax.broadcasted_iota(jnp.int32, (1, block), 1)
        out_ref[...] = jnp.where(slots < used, orb, 0.0).astype(BF16)

    @pl.when(first >= used)
    def _():
        out_ref[...] = jnp.zeros_like(out_ref)


def edges(src, dst, used, table, own, send_w, recv_w, mapping):
    e_dev = src.shape[0]
    orbitals, chans = mapping.shape
    block = min(512, e_dev)
    whole = pl.BlockSpec(memory_space=pltpu.VMEM)
    scalars = pl.BlockSpec(memory_space=pltpu.SMEM)
    return pl.pallas_call(
        edges_kernel,
        grid=(e_dev // block,),
        in_specs=[scalars, scalars, scalars, whole, whole, whole, whole, whole],
        out_specs=pl.BlockSpec((orbitals, block), lambda i: (0, i)),
        out_shape=jax.ShapeDtypeStruct((orbitals, e_dev), BF16),
        scratch_shapes=[
            pltpu.VMEM((table.shape[0], chans), F32),
            pltpu.VMEM((own.shape[0], chans), F32),
            pltpu.VMEM((block, chans), F32),
        ],
        compiler_params=pltpu.CompilerParams(vmem_limit_bytes=48 * 1024 * 1024),
        name="edges",
    )(src, dst, used, table, own, send_w, recv_w, mapping)


def from_behind(array, axis, by):
    devices = lax.axis_size(axis)
    return lax.ppermute(array, axis, [(i, (i + by) % devices) for i in range(devices)])


def strides(devices):
    found, stride = [], 1
    for size in (2, 2):
        if devices % (stride * size) == 0 and devices > stride:
            found.append((stride, size))
            stride *= size
    if devices > stride:
        found.append((stride, devices // stride))
    return found


def shifted(array, devices, stride, size, by):
    pairs = []
    for i in range(devices):
        place = (i // stride) % size
        pairs.append((i, i + ((place + by) % size - place) * stride))
    return lax.ppermute(array, "atoms", pairs)


def sum_stage(array, dim, stride, size):
    devices = lax.axis_size("atoms")
    place = (lax.axis_index("atoms") // stride) % size
    part = array.shape[dim] // size
    total = lax.dynamic_slice_in_dim(array, place * part, part, dim).astype(F32)
    for by in range(1, size):
        away = lax.rem(place + by, size)
        piece = lax.dynamic_slice_in_dim(array, away * part, part, dim)
        total = total + shifted(piece, devices, stride, size, by).astype(F32)
    return total


def part_start(total):
    devices = lax.axis_size("atoms")
    me = lax.axis_index("atoms")
    start = 0
    for stride, size in strides(devices):
        total = total // size
        start = start + ((me // stride) % size) * total
    return start


def gather_stage(array, dim, stride, size):
    devices = lax.axis_size("atoms")
    place = (lax.axis_index("atoms") // stride) % size
    part = array.shape[dim]
    shape = list(array.shape)
    shape[dim] = part * size
    whole = lax.dynamic_update_slice_in_dim(jnp.zeros(shape, array.dtype), array, place * part, dim)
    for by in range(1, size):
        came = lax.rem(place - by + size, size)
        moved = shifted(array, devices, stride, size, by)
        whole = lax.dynamic_update_slice_in_dim(whole, moved, came * part, dim)
    return whole


def structure_stages(own_filter, norm_scale):
    factors = strides(lax.axis_size("atoms"))
    steps = []
    for n, (stride, size) in enumerate(factors):
        def add(array, stride=stride, size=size, last=n == len(factors) - 1):
            total = sum_stage(array, 1, stride, size)
            if last:
                total = own_filter[None] * total * norm_scale
            return total.astype(BF16)

        steps.append(add)
    for stride, size in reversed(factors):
        steps.append(lambda array, stride=stride, size=size: gather_stage(array, 1, stride, size))
    return steps


def finish_rows(feat_rows, update, gain):
    refreshed = feat_rows.astype(F32) + jax.nn.silu(update)
    scaled = refreshed * lax.rsqrt(jnp.mean(refreshed * refreshed, axis=-1, keepdims=True) + 1e-06)
    return (scaled * gain).astype(BF16)


def local(
    particle_traits,
    particle_coordinates,
    kspace_vectors,
    learned_kspace_filter,
    spatial_home,
    following_halo_lines,
    previous_halo_lines,
    sender_projection,
    receiver_projection,
    pair_channel_mapping,
    vertex_rescaling_gain,
    link_sender_line,
    link_receiver_particle,
    active_link_tally,
):
    n_atoms = lax.axis_size("atoms")
    kspace_tally = lax.axis_size("kvec")
    a_dev, chans = particle_traits.shape
    group = a_dev // n_atoms
    sub_rows = group // kspace_tally
    kspace = kspace_vectors.shape[1]
    norm_scale = 1.0 / math.sqrt(a_dev * n_atoms * kspace * kspace_tally)

    pieces = 4
    padded = jnp.concatenate([particle_coordinates, jnp.zeros((8 - particle_coordinates.shape[0], a_dev), F32)], axis=0)
    k_turns = (kspace_vectors * (0.5 / math.pi)).T

    share = sub_rows // pieces
    count = a_dev // pieces
    within = spatial_home % sub_rows
    places = (within // share) * count + (spatial_home // sub_rows) * share + within % share
    kvec_index = lax.axis_index("kvec")

    k_part = kspace // 2
    made = {}

    def waves_of(half, n, k):
        k_half = lax.slice_in_dim(k, half * k_part, (half + 1) * k_part)
        made[half, n] = wave_sums(k_half, placed[n][1], placed[n][0])

    def sums_of(half):
        return sum(made[half, n][0].astype(F32) for n in range(pieces)).astype(BF16)

    placed = [sort_atoms(places, padded, particle_traits, n * count, count) for n in range(pieces)]
    steps = []
    for half in range(2):
        own_filter = lax.dynamic_slice_in_dim(
            learned_kspace_filter, half * k_part + part_start(k_part), k_part // n_atoms, 0
        )
        steps.append(structure_stages(own_filter, norm_scale))
    for n in range(pieces):
        waves_of(0, n, k_turns)
    state = sums_of(0)
    for n in range(pieces):
        state, k_turns = lax.optimization_barrier((state, k_turns))
        waves_of(1, n, k_turns)
        state = steps[0][n](state)
        state, k_turns, made[1, n] = lax.optimization_barrier((state, k_turns, made[1, n]))
    last = sums_of(1)
    for turn in range(len(steps[1])):
        last = steps[1][turn](last)
        if turn + pieces < len(steps[0]):
            state = steps[0][turn + pieces](state)
    filts = [state, last]

    updates, feats = [], []
    for n in range(pieces):
        partial = update_rows(filts, [made[half, n][1:] for half in range(2)])
        partial = partial.reshape(n_atoms, kspace_tally, share, chans)
        update = [lax.dynamic_index_in_dim(partial, kvec_index, 1, False)]
        for by in range(1, kspace_tally):
            away = lax.rem(kvec_index + by, kspace_tally)
            piece = lax.dynamic_index_in_dim(partial, away, 1, False)
            update.append(from_behind(piece, "kvec", by))
        updates.append(update)
        feat = placed[n][0].reshape(n_atoms, kspace_tally, share, chans)
        feats.append(lax.dynamic_index_in_dim(feat, kvec_index, 1, False))
    for n in range(pieces - 1):
        updates[n], updates[n + 1][0] = lax.optimization_barrier((updates[n], updates[n + 1][0]))
    partition_rows = jnp.zeros((n_atoms, kspace_tally, pieces, share, chans), BF16)
    arrived = None
    for n in range(pieces):
        update = updates[n]
        if n:
            update, arrived = lax.optimization_barrier((update, arrived))
        update = sum(term.astype(F32) for term in update)
        node = finish_rows(feats[n], update, vertex_rescaling_gain)
        arrived = lax.all_to_all(node, "atoms", split_axis=0, concat_axis=0, tiled=True)
        for by in range(kspace_tally):
            came = lax.rem(kvec_index - by + kspace_tally, kspace_tally)
            moved = arrived if by == 0 else from_behind(arrived, "kvec", by)
            partition_rows = lax.dynamic_update_slice(
                partition_rows, moved[:, None, None], (0, came, n, 0, 0)
            )
    partition_rows = partition_rows.reshape(a_dev, chans)
    from_lower = from_behind(partition_rows[following_halo_lines[0]], "atoms", 1)
    from_upper = from_behind(partition_rows[previous_halo_lines[0]], "atoms", -1)
    row_table = jnp.concatenate([partition_rows, from_lower, from_upper], axis=0)
    orbital_blocks = edges(
        link_sender_line,
        link_receiver_particle,
        active_link_tally,
        row_table,
        partition_rows,
        sender_projection,
        receiver_projection,
        pair_channel_mapping,
    )
    return (orbital_blocks, partition_rows)


def solution(mesh):
    placed = (
        P("atoms", None),
        P(None, "atoms"),
        P(None, "kvec"),
        P("kvec", None),
        P("atoms", None),
        P("atoms", None),
        P("atoms", None),
        P(),
        P(),
        P(),
        P(),
        P(("atoms", "kvec")),
        P(("atoms", "kvec")),
        P(("atoms", "kvec")),
    )
    return jax.shard_map(
        local,
        mesh=mesh,
        in_specs=placed,
        out_specs=(P(None, ("atoms", "kvec")), P("atoms", None)),
        check_vma=False,
    )
```
